32 devices in a mesh: dp: 4 (over y, x), expert: 8 (over z, core).
Axes of the slice: x: 2, y: 2, z: 4, core: 2. Of those that a mesh axis runs over, the one named last changes fastest.
Arguments:
- tokens: bfloat16 [8192, 4096], P(('dp', 'expert')), may hold values from -6 to 6
- latent_down: bfloat16 [4096, 1024], P(('dp', 'expert')), may hold values from -0.09375 to 0.09375
- latent_up: bfloat16 [1024, 4096], P(('dp', 'expert')), may hold values from -0.1875 to 0.1875
- expert_gate: bfloat16 [32, 1024, 2048], P('expert', None, 'dp'), may hold values from -0.1875 to 0.1875
- expert_up: bfloat16 [32, 1024, 2048], P('expert', None, 'dp'), may hold values from -0.1875 to 0.1875
- expert_down: bfloat16 [32, 2048, 1024], P('expert', 'dp'), may hold values from -0.125 to 0.125
- chosen_experts: int32 [8192, 4], P(('dp', 'expert')), may hold values from 0 to 31, all different within a row
- combine_weights: float32 [8192, 4], P(('dp', 'expert')), may hold values from 0.1 to 0.6
- capacity: int32 [32], replicated, may hold values from 16 to 32, as said below
- fallback: int32 [32, 128], P(('dp', 'expert')), may hold values from 0 to 31, as said below
Outputs:
- mixed: bfloat16 [8192, 4096], P(('dp', 'expert'))
The draws below stay inside these ranges and needn't reach their ends.
Inputs may be any that keep to these rules, and one draw needn't show every extreme that they name: capacity is at most 32, and equals 32 for some expert. fallback[b, o] // 4 equals o modulo 32 // 4. `chosen_experts`: the 4 experts of one token differ.
All inputs are finite; a program needn't handle non-finite values.
Results may differ from the reference program's by a relative error of at most 0.014.
Values may be sent and summed in bfloat16 or wider, within the bound.
A program may use at most 128 MiB of HBM per device.

```python
import jax
import jax.numpy as jnp
from jax import lax

D = 4096
LATENT = 1024
FF = 2048
EXP_DEV = 4
TOP = 4
TOK_DEV = 256
EXPERTS = 32
TOKENS = 8192
BLOCKS = 32
CAP = 32
SP_PEER = 16
SPILL = 128
FF_DEV = 512
N_DP = 4


def draw_capacity(key, part):
    key = jax.random.fold_in(key, 11)
    low_cap = CAP - CAP // 2
    values = jax.random.randint(key, (EXPERTS,), low_cap, CAP + 1, dtype=jnp.int32)
    shuffled = jax.random.permutation(jax.random.fold_in(key, 1), EXPERTS)
    values = values.at[shuffled[0]].set(CAP).at[shuffled[1]].set(low_cap)
    return values.astype(jnp.int32)


def draw_fallback(key, part):
    key = jax.random.fold_in(key, 23)
    local_pick = jax.random.randint(key, (BLOCKS, SPILL), 0, EXP_DEV, dtype=jnp.int32)
    local_pick = local_pick.at[0, 0].set(0).at[0, SPILL - 1].set(EXP_DEV - 1)
    peer_count = EXPERTS // EXP_DEV
    peer_index = jnp.arange(SPILL, dtype=jnp.int32) % peer_count
    return (peer_index[None, :] * EXP_DEV + local_pick).astype(jnp.int32)


def block_scale(own_key, shape, shards, least, largest):
    def one(axis_at, shards_of):
        heights = jax.random.uniform(jax.random.fold_in(jax.random.fold_in(own_key, 6), axis_at), (shards_of,), jnp.float32, least / len(shards), largest / len(shards))
        return jnp.repeat(jnp.exp(heights), shape[axis_at] // shards_of).reshape((-1,) + (1,) * (len(shape) - axis_at - 1))

    factor_of = one(*shards[0])
    for cut in shards[1:]:
        factor_of = factor_of * one(*cut)
    return factor_of


def choose_distinct(stream_key, rows, amount, top, lift):
    order = jax.random.permutation(jax.random.fold_in(stream_key, 1), amount)
    pull = order
    for power in range(3):
        pull = pull * pull // amount
    pull = pull * lift // amount
    lots = jax.random.randint(jax.random.fold_in(stream_key, 2), (rows, amount), 0, 4096) + pull
    sure = jax.random.permutation(jax.random.fold_in(stream_key, 3), rows)[jnp.arange(amount) % rows]
    lots = jnp.where(jnp.arange(rows)[:, None] == sure[None, :], 1 << 14, lots)
    score = lots * amount + jnp.arange(amount)
    return lax.top_k(score.astype(jnp.int32), top)[1].astype(jnp.int32)


def noise(stream_key, shape, width, limit, cuts=(), kind=jnp.bfloat16):
    values = width * jax.random.normal(stream_key, shape, jnp.float32)
    if cuts:
        values = values * block_scale(stream_key, shape, cuts, -0.22, 0.18)
    return jnp.clip(values, -limit, limit).astype(kind)


def setup_inputs(seed: int = 0) -> dict:
    seeds = jax.random.split(jax.random.key(seed), 11)
    tokens = noise(seeds[0], (TOKENS, D), 1.0, 6.0, ((0, 32),))
    latent_down = noise(seeds[1], (D, LATENT), D ** -0.5, 0.09375, ((0, 32),))
    latent_up = noise(seeds[2], (LATENT, D), LATENT ** -0.5, 0.1875, ((0, 32),))
    expert_gate = noise(seeds[3], (EXPERTS, LATENT, FF), LATENT ** -0.5, 0.1875, ((0, 8), (2, 4)))
    expert_up = noise(seeds[4], (EXPERTS, LATENT, FF), LATENT ** -0.5, 0.1875, ((0, 8), (2, 4)))
    expert_down = noise(seeds[5], (EXPERTS, FF, LATENT), FF ** -0.5, 0.125, ((0, 8), (1, 4)))
    chosen_experts = choose_distinct(seeds[6], TOKENS, EXPERTS, TOP, 1024)
    combine_weights = jnp.clip(0.1 + 0.5 * jax.random.uniform(seeds[7], (TOKENS, TOP), jnp.float32) ** block_scale(seeds[7], (TOKENS, TOP), ((0, 32),), -0.2, 0.2), 0.1, 0.6)
    capacity = draw_capacity(jax.random.fold_in(seeds[10], 71), 0)
    fallback = draw_fallback(jax.random.fold_in(seeds[10], 71), 0)
    return dict(tokens=tokens, latent_down=latent_down, latent_up=latent_up, expert_gate=expert_gate, expert_up=expert_up, expert_down=expert_down, chosen_experts=chosen_experts, combine_weights=combine_weights, capacity=capacity, fallback=fallback)


def assign_slots(block_experts, capacity, local_experts, slot_cap, spill_peer, peer_count):
    flat_experts = block_experts.reshape(-1).astype(jnp.int32)
    expert_count = capacity.shape[0]
    onehot = (flat_experts[:, None] == jnp.arange(expert_count, dtype=jnp.int32)[None, :]).astype(jnp.int32)
    earlier = (jnp.cumsum(onehot, axis=0) - onehot).astype(jnp.int32)
    slot_rank = jnp.sum(earlier * onehot, axis=1).astype(jnp.int32)
    slot_limit = jnp.sum(onehot * capacity[None, :].astype(jnp.int32), axis=1).astype(jnp.int32)
    is_main = slot_rank < slot_limit
    overflow = jnp.where(is_main, 0, 1).astype(jnp.int32)
    spill_number = (jnp.cumsum(overflow) - overflow).astype(jnp.int32)
    rows_peer = local_experts * slot_cap + spill_peer
    main_slot = (flat_experts // local_experts) * rows_peer + (flat_experts % local_experts) * slot_cap + slot_rank
    spill_slot = (spill_number % peer_count) * rows_peer + local_experts * slot_cap + spill_number // peer_count
    outside = peer_count * rows_peer
    in_spill = spill_number < spill_peer * peer_count
    return jnp.where(is_main, main_slot, jnp.where(in_spill, spill_slot, outside)).astype(jnp.int32)


def expert_output(rows, gate_weight, up_weight, down_weight):
    gate_value = jnp.dot(rows, gate_weight, preferred_element_type=jnp.float32)
    up_value = jnp.dot(rows, up_weight, preferred_element_type=jnp.float32)
    hidden = (jax.nn.silu(gate_value) * up_value).astype(jnp.bfloat16)
    running = jnp.zeros((rows.shape[0], down_weight.shape[1]), jnp.float32)
    for quarter in range(N_DP):
        lower_unit = quarter * FF_DEV
        part_sum = jnp.dot(hidden[:, lower_unit:lower_unit + FF_DEV], down_weight[lower_unit:lower_unit + FF_DEV], preferred_element_type=jnp.float32)
        rounded = lax.optimization_barrier(part_sum.astype(jnp.bfloat16))
        running = running + rounded.astype(jnp.float32)
    return running.astype(jnp.bfloat16)


def reference(tokens, latent_down, latent_up, expert_gate, expert_up, expert_down, chosen_experts, combine_weights, capacity, fallback):
    peer_count = EXPERTS // EXP_DEV
    rows_peer = EXP_DEV * CAP + SP_PEER
    main_width = EXP_DEV * CAP
    latent = jnp.dot(tokens, latent_down, preferred_element_type=jnp.float32).astype(jnp.bfloat16)
    latent_blocks = latent.reshape(BLOCKS, TOK_DEV, LATENT)
    expert_blocks = chosen_experts.reshape(BLOCKS, TOK_DEV, TOP)
    weight_blocks = combine_weights.reshape(BLOCKS, TOK_DEV, TOP)

    def dispatch(block):
        latent_rows, block_experts, block_fallback = block
        slot_index = assign_slots(block_experts, capacity, EXP_DEV, CAP, SP_PEER, peer_count)
        source_rows = jnp.repeat(latent_rows, TOP, axis=0)
        buffer = jnp.zeros((peer_count * rows_peer, LATENT), jnp.bfloat16).at[slot_index].set(source_rows, mode="drop")
        owner = (block_fallback.reshape(SP_PEER, peer_count).T % EXP_DEV).astype(jnp.int32)
        return buffer.reshape(peer_count, rows_peer, LATENT), owner

    buffers, owners = lax.map(dispatch, (latent_blocks, expert_blocks, fallback))
    grouped_rows = jnp.transpose(buffers, (1, 0, 2, 3))
    grouped_owner = jnp.transpose(owners, (1, 0, 2))
    gate_groups = expert_gate.reshape(peer_count, EXP_DEV, LATENT, FF)
    up_groups = expert_up.reshape(peer_count, EXP_DEV, LATENT, FF)
    down_groups = expert_down.reshape(peer_count, EXP_DEV, FF, LATENT)

    def serve(group):
        rows_group, owner_group, gate_group, up_group, down_group = group
        main_rows = rows_group[:, :main_width].reshape(BLOCKS, EXP_DEV, CAP, LATENT)
        spill_rows = rows_group[:, main_width:]
        main_parts = []
        spill_sum = jnp.zeros((BLOCKS * SP_PEER, LATENT), jnp.float32)
        for local_index in range(EXP_DEV):
            main_in = main_rows[:, local_index].reshape(BLOCKS * CAP, LATENT)
            main_result = expert_output(main_in, gate_group[local_index], up_group[local_index], down_group[local_index])
            main_parts.append(main_result.reshape(BLOCKS, 1, CAP, LATENT))
            chosen = (owner_group == local_index)[:, :, None]
            masked = jnp.where(chosen, spill_rows, jnp.zeros_like(spill_rows)).reshape(BLOCKS * SP_PEER, LATENT)
            spill_result = expert_output(masked, gate_group[local_index], up_group[local_index], down_group[local_index])
            spill_sum = spill_sum + spill_result.astype(jnp.float32)
        main_out = jnp.concatenate(main_parts, axis=1).reshape(BLOCKS, main_width, LATENT)
        spill_out = spill_sum.astype(jnp.bfloat16).reshape(BLOCKS, SP_PEER, LATENT)
        return jnp.concatenate([main_out, spill_out], axis=1)

    served = lax.map(serve, (grouped_rows, grouped_owner, gate_groups, up_groups, down_groups))
    outputs = jnp.transpose(served, (1, 0, 2, 3))

    def combine(block):
        block_outputs, block_experts, block_weights = block
        slot_index = assign_slots(block_experts, capacity, EXP_DEV, CAP, SP_PEER, peer_count)
        picked = jnp.take(block_outputs.reshape(peer_count * rows_peer, LATENT), slot_index, axis=0, mode="fill", fill_value=0)
        weighted = picked.reshape(TOK_DEV, TOP, LATENT).astype(jnp.float32) * block_weights[:, :, None].astype(jnp.float32)
        return jnp.sum(weighted, axis=1).astype(jnp.bfloat16)

    combined = lax.map(combine, (outputs, expert_blocks, weight_blocks)).reshape(TOKENS, LATENT)
    return jnp.dot(combined, latent_up, preferred_element_type=jnp.float32).astype(jnp.bfloat16)
```

```python
import jax
import jax.numpy as jnp
from jax import lax
from jax.sharding import Mesh
from jax.sharding import PartitionSpec as P

ALL = ("dp", "pair", "core")
PLANE = ("dp", "pair")


def dot32(a, b):
    return jnp.dot(a, b, preferred_element_type=jnp.float32)


def place_rows(block_experts, capacity, fallback, local_experts, slot_cap, spill_peer, peer_count):
    flat_experts = block_experts.reshape(-1)
    expert_count = capacity.shape[0]
    onehot = (flat_experts[:, None] == jnp.arange(expert_count, dtype=jnp.int32)[None, :]).astype(
        jnp.int32
    )
    earlier = jnp.cumsum(onehot, axis=0) - onehot
    slot_rank = jnp.sum(earlier * onehot, axis=1)
    slot_limit = jnp.sum(onehot * capacity[None, :], axis=1)
    is_main = slot_rank < slot_limit
    overflow = jnp.where(is_main, 0, 1).astype(jnp.int32)
    spill_number = jnp.cumsum(overflow) - overflow
    spill_all = spill_peer * peer_count
    in_spill = spill_number < spill_all
    number_hot = spill_number[:, None] == jnp.arange(spill_all, dtype=jnp.int32)[None, :]
    spill_target = jnp.sum(jnp.where(number_hot, fallback.reshape(1, -1), 0), axis=1)
    target = jnp.where(is_main, flat_experts, spill_target)
    slot = jnp.where(is_main, slot_rank, slot_cap + spill_number // peer_count)
    slot_width = slot_cap + spill_peer
    row = ((target % local_experts) * peer_count + target // local_experts) * slot_width + slot
    outside = local_experts * peer_count * slot_width
    return jnp.where(is_main | in_spill, row, outside).reshape(block_experts.shape)


def on_device(
    tokens,
    latent_down,
    latent_up,
    expert_gate,
    expert_up,
    expert_down,
    chosen_experts,
    combine_weights,
    capacity,
    fallback,
):
    tok_count = tokens.shape[0]
    latent_width = expert_gate.shape[1]
    local_experts = expert_gate.shape[0]
    top_count = chosen_experts.shape[1]
    peer_count = lax.axis_size("pair") * lax.axis_size("core")
    team_size = lax.axis_size("dp")
    expert_count = capacity.shape[0]
    spill_peer = fallback.shape[1] // peer_count
    slot_cap = tok_count * top_count // expert_count
    slot_width = slot_cap + spill_peer
    row_count = local_experts * peer_count * slot_width
    team = lax.axis_index("dp")
    core = lax.axis_index("core")

    def swap(value):
        return lax.ppermute(value, "core", [(0, 1), (1, 0)])

    def ordered(mine, other, axis):
        first = jnp.where(core == 0, mine, other)
        second = jnp.where(core == 0, other, mine)
        return jnp.concatenate([first, second], axis=axis)

    def column_half(shard):
        half = shard.shape[1] // 2
        mine = lax.dynamic_slice_in_dim(shard, core * half, half, 1)
        other = swap(lax.dynamic_slice_in_dim(shard, (1 - core) * half, half, 1))
        return lax.all_gather(ordered(mine, other, 0), PLANE, axis=0, tiled=True)

    down_half = column_half(latent_down)
    partner_tokens = swap(tokens)

    blocks = []
    for shift in range(team_size):
        partner = jnp.bitwise_xor(team, shift)
        gate, up, down = (
            lax.dynamic_index_in_dim(w, partner, 0, keepdims=False)
            for w in (expert_gate, expert_up, expert_down)
        )
        part = jnp.concatenate([jnp.concatenate([gate, up], axis=1), down], axis=0)
        if shift:
            part = lax.ppermute(part, "dp", [(d, d ^ shift) for d in range(team_size)])
        blocks.append(part)

    rows_of = place_rows(
        chosen_experts, capacity, fallback, local_experts, slot_cap, spill_peer, peer_count
    )
    hit = rows_of[:, :, None] == jnp.arange(row_count, dtype=jnp.int32)[None, None, :]
    spread = jnp.any(hit, axis=1).astype(jnp.bfloat16)
    weight = jnp.sum(jnp.where(hit, combine_weights[:, :, None], 0.0), axis=1)
    weight_high = weight.astype(jnp.bfloat16)
    weight_low = (weight - weight_high.astype(jnp.float32)).astype(jnp.bfloat16)

    for_partner = dot32(partner_tokens, down_half).astype(jnp.bfloat16)
    from_partner = swap(for_partner)
    for_me = dot32(tokens, down_half).astype(jnp.bfloat16)
    latent = ordered(for_me, from_partner, 1)
    outgoing = lax.dot_general(
        spread, latent, (((0,), (0,)), ((), ())), preferred_element_type=jnp.float32
    ).astype(jnp.bfloat16)
    outgoing = outgoing.reshape(local_experts * peer_count, slot_width, latent_width)
    outgoing, latent_up = lax.optimization_barrier((outgoing, latent_up))
    arrived = lax.all_to_all(outgoing, ALL, split_axis=0, concat_axis=0, tiled=True)
    rows = arrived.reshape(-1, latent_width)

    total = jnp.zeros((row_count, latent_width), jnp.float32)
    units = expert_down.shape[1]
    for part in blocks:
        both = dot32(rows, part[:latent_width])
        hidden = (jax.nn.silu(both[:, :units]) * both[:, units:]).astype(jnp.bfloat16)
        total = total + dot32(hidden, part[latent_width:]).astype(jnp.bfloat16).astype(jnp.float32)
    served = total.astype(jnp.bfloat16).reshape(local_experts * peer_count, slot_width, latent_width)
    back = lax.all_to_all(served, ALL, split_axis=0, concat_axis=0, tiled=True)
    back = back.reshape(row_count, latent_width)
    combined = (dot32(weight_high, back) + dot32(weight_low, back)).astype(jnp.bfloat16)

    up_half = column_half(latent_up)
    up_whole = ordered(up_half, swap(up_half), 1)
    return dot32(combined, up_whole).astype(jnp.bfloat16)


def solution(mesh):
    teams, peers = mesh.devices.shape
    split = Mesh(mesh.devices.reshape(teams, peers // 2, 2), ALL)
    experts = ("pair", "core")
    mapped = jax.shard_map(
        on_device,
        mesh=split,
        in_specs=(
            P(ALL, None),
            P(ALL, None),
            P(ALL, None),
            P(experts, None, "dp"),
            P(experts, None, "dp"),
            P(experts, "dp", None),
            P(ALL, None),
            P(ALL, None),
            P(),
            P(ALL, None),
        ),
        out_specs=P(ALL, None),
        check_vma=False,
    )
    return mapped
```

```python
import jax
import jax.numpy as jnp
from jax import lax
from jax.sharding import Mesh
from jax.sharding import PartitionSpec as P

ALL = ("dp", "pair", "core")
PLANE = ("dp", "pair")


def dot32(a, b):
    return jnp.dot(a, b, preferred_element_type=jnp.float32)


def place_rows(block_experts, capacity, fallback, local_experts, slot_cap, spill_peer, peer_count):
    flat_experts = block_experts.reshape(-1)
    expert_count = capacity.shape[0]
    onehot = (flat_experts[:, None] == jnp.arange(expert_count, dtype=jnp.int32)[None, :]).astype(
        jnp.int32
    )
    earlier = jnp.cumsum(onehot, axis=0) - onehot
    slot_rank = jnp.sum(earlier * onehot, axis=1)
    slot_limit = jnp.sum(onehot * capacity[None, :], axis=1)
    is_main = slot_rank < slot_limit
    overflow = jnp.where(is_main, 0, 1).astype(jnp.int32)
    spill_number = jnp.cumsum(overflow) - overflow
    spill_all = spill_peer * peer_count
    in_spill = spill_number < spill_all
    number_hot = spill_number[:, None] == jnp.arange(spill_all, dtype=jnp.int32)[None, :]
    spill_target = jnp.sum(jnp.where(number_hot, fallback.reshape(1, -1), 0), axis=1)
    target = jnp.where(is_main, flat_experts, spill_target)
    slot = jnp.where(is_main, slot_rank, slot_cap + spill_number // peer_count)
    slot_width = slot_cap + spill_peer
    row = ((target % local_experts) * peer_count + target // local_experts) * slot_width + slot
    outside = local_experts * peer_count * slot_width
    return jnp.where(is_main | in_spill, row, outside).reshape(block_experts.shape)


def on_device(
    tokens,
    latent_down,
    latent_up,
    expert_gate,
    expert_up,
    expert_down,
    chosen_experts,
    combine_weights,
    capacity,
    fallback,
):
    tok_count = tokens.shape[0]
    latent_width = expert_gate.shape[1]
    local_experts = expert_gate.shape[0]
    top_count = chosen_experts.shape[1]
    peer_count = lax.axis_size("pair") * lax.axis_size("core")
    team_size = lax.axis_size("dp")
    expert_count = capacity.shape[0]
    spill_peer = fallback.shape[1] // peer_count
    slot_cap = tok_count * top_count // expert_count
    slot_width = slot_cap + spill_peer
    row_count = local_experts * peer_count * slot_width
    team = lax.axis_index("dp")
    core = lax.axis_index("core")

    def swap(value):
        return lax.ppermute(value, "core", [(0, 1), (1, 0)])

    def ordered(mine, other, axis):
        first = jnp.where(core == 0, mine, other)
        second = jnp.where(core == 0, other, mine)
        return jnp.concatenate([first, second], axis=axis)

    def column_half(shard):
        half = shard.shape[1] // 2
        mine = lax.dynamic_slice_in_dim(shard, core * half, half, 1)
        other = swap(lax.dynamic_slice_in_dim(shard, (1 - core) * half, half, 1))
        return lax.all_gather(ordered(mine, other, 0), PLANE, axis=0, tiled=True)

    down_half = column_half(latent_down)
    partner_tokens = swap(tokens)

    blocks = []
    for shift in range(team_size):
        partner = jnp.bitwise_xor(team, shift)
        gate, up, down = (
            lax.dynamic_index_in_dim(w, partner, 0, keepdims=False)
            for w in (expert_gate, expert_up, expert_down)
        )
        part = jnp.concatenate([jnp.concatenate([gate, up], axis=1), down], axis=0)
        blocks.append(part)

    def exchange(shift):
        pairs = [(d, d ^ shift) for d in range(team_size)]
        return lax.ppermute(blocks[shift], "dp", pairs)

    early = range(1, team_size - 1)
    tied = lax.optimization_barrier((down_half, blocks[-1], *[exchange(s) for s in early]))
    down_half, blocks[-1] = tied[:2]
    blocks[1:-1] = tied[2:]
    blocks[-1] = exchange(team_size - 1)

    rows_of = place_rows(
        chosen_experts, capacity, fallback, local_experts, slot_cap, spill_peer, peer_count
    )
    hit = rows_of[:, :, None] == jnp.arange(row_count, dtype=jnp.int32)[None, None, :]
    spread = jnp.any(hit, axis=1).astype(jnp.bfloat16)
    weight = jnp.sum(jnp.where(hit, combine_weights[:, :, None], 0.0), axis=1)
    weight_high = weight.astype(jnp.bfloat16)
    weight_low = (weight - weight_high.astype(jnp.float32)).astype(jnp.bfloat16)

    for_partner = dot32(partner_tokens, down_half).astype(jnp.bfloat16)
    from_partner = swap(for_partner)
    for_me = dot32(tokens, down_half).astype(jnp.bfloat16)
    latent = ordered(for_me, from_partner, 1)
    outgoing = lax.dot_general(
        spread, latent, (((0,), (0,)), ((), ())), preferred_element_type=jnp.float32
    ).astype(jnp.bfloat16)
    outgoing = outgoing.reshape(local_experts * peer_count, slot_width, latent_width)
    arrived = lax.all_to_all(outgoing, ALL, split_axis=0, concat_axis=0, tiled=True)
    arrived, latent_up = lax.optimization_barrier((arrived, latent_up))
    rows = arrived.reshape(-1, latent_width)

    total = jnp.zeros((row_count, latent_width), jnp.float32)
    units = expert_down.shape[1]
    for part in blocks:
        both = dot32(rows, part[:latent_width])
        hidden = (jax.nn.silu(both[:, :units]) * both[:, units:]).astype(jnp.bfloat16)
        total = total + dot32(hidden, part[latent_width:]).astype(jnp.bfloat16).astype(jnp.float32)
    served = total.astype(jnp.bfloat16).reshape(local_experts * peer_count, slot_width, latent_width)
    back = lax.all_to_all(served, ALL, split_axis=0, concat_axis=0, tiled=True)
    up_half = column_half(latent_up)
    up_whole = ordered(up_half, swap(up_half), 1)
    back, up_whole = lax.optimization_barrier((back, up_whole))
    back = back.reshape(row_count, latent_width)
    combined = (dot32(weight_high, back) + dot32(weight_low, back)).astype(jnp.bfloat16)

    return dot32(combined, up_whole).astype(jnp.bfloat16)


def solution(mesh):
    teams, peers = mesh.devices.shape
    split = Mesh(mesh.devices.reshape(teams, peers // 2, 2), ALL)
    experts = ("pair", "core")
    mapped = jax.shard_map(
        on_device,
        mesh=split,
        in_specs=(
            P(ALL, None),
            P(ALL, None),
            P(ALL, None),
            P(experts, None, "dp"),
            P(experts, None, "dp"),
            P(experts, "dp", None),
            P(ALL, None),
            P(ALL, None),
            P(),
            P(ALL, None),
        ),
        out_specs=P(ALL, None),
        check_vma=False,
    )
    return mapped
```

```python
import jax
import jax.numpy as jnp
from jax import lax
from jax.sharding import Mesh
from jax.sharding import PartitionSpec as P

ALL = ("dp", "pair", "core")
PLANE = ("dp", "pair")


def dot32(a, b):
    return jnp.dot(a, b, preferred_element_type=jnp.float32)


def place_rows(block_experts, capacity, fallback, local_experts, slot_cap, spill_peer, peer_count):
    flat_experts = block_experts.reshape(-1)
    expert_count = capacity.shape[0]
    onehot = (flat_experts[:, None] == jnp.arange(expert_count, dtype=jnp.int32)[None, :]).astype(
        jnp.int32
    )
    earlier = jnp.cumsum(onehot, axis=0) - onehot
    slot_rank = jnp.sum(earlier * onehot, axis=1)
    slot_limit = jnp.sum(onehot * capacity[None, :], axis=1)
    is_main = slot_rank < slot_limit
    overflow = jnp.where(is_main, 0, 1).astype(jnp.int32)
    spill_number = jnp.cumsum(overflow) - overflow
    spill_all = spill_peer * peer_count
    in_spill = spill_number < spill_all
    number_hot = spill_number[:, None] == jnp.arange(spill_all, dtype=jnp.int32)[None, :]
    spill_target = jnp.sum(jnp.where(number_hot, fallback.reshape(1, -1), 0), axis=1)
    target = jnp.where(is_main, flat_experts, spill_target)
    slot = jnp.where(is_main, slot_rank, slot_cap + spill_number // peer_count)
    slot_width = slot_cap + spill_peer
    row = ((target % local_experts) * peer_count + target // local_experts) * slot_width + slot
    outside = local_experts * peer_count * slot_width
    return jnp.where(is_main | in_spill, row, outside).reshape(block_experts.shape)


def on_device(
    tokens,
    latent_down,
    latent_up,
    expert_gate,
    expert_up,
    expert_down,
    chosen_experts,
    combine_weights,
    capacity,
    fallback,
):
    tok_count = tokens.shape[0]
    latent_width = expert_gate.shape[1]
    local_experts = expert_gate.shape[0]
    top_count = chosen_experts.shape[1]
    peer_count = lax.axis_size("pair") * lax.axis_size("core")
    team_size = lax.axis_size("dp")
    expert_count = capacity.shape[0]
    spill_peer = fallback.shape[1] // peer_count
    slot_cap = tok_count * top_count // expert_count
    slot_width = slot_cap + spill_peer
    row_count = local_experts * peer_count * slot_width
    team = lax.axis_index("dp")
    core = lax.axis_index("core")

    def swap(value):
        return lax.ppermute(value, "core", [(0, 1), (1, 0)])

    def ordered(mine, other, axis):
        first = jnp.where(core == 0, mine, other)
        second = jnp.where(core == 0, other, mine)
        return jnp.concatenate([first, second], axis=axis)

    def column_half(shard):
        half = shard.shape[1] // 2
        mine = lax.dynamic_slice_in_dim(shard, core * half, half, 1)
        other = swap(lax.dynamic_slice_in_dim(shard, (1 - core) * half, half, 1))
        return ordered(mine, other, 0)

    def gather(half):
        return lax.all_gather(half, PLANE, axis=0, tiled=True)

    down_half = gather(column_half(latent_down))
    up_pair = column_half(latent_up)
    partner_tokens = swap(tokens)

    blocks = []
    for shift in range(team_size):
        partner = jnp.bitwise_xor(team, shift)
        gate, up, down = (
            lax.dynamic_index_in_dim(w, partner, 0, keepdims=False)
            for w in (expert_gate, expert_up, expert_down)
        )
        part = jnp.concatenate([jnp.concatenate([gate, up], axis=1), down], axis=0)
        blocks.append(part)

    def exchange(shift):
        pairs = [(d, d ^ shift) for d in range(team_size)]
        return lax.ppermute(blocks[shift], "dp", pairs)

    early = range(1, team_size - 1)
    tied = lax.optimization_barrier((down_half, blocks[-1], *[exchange(s) for s in early]))
    down_half, blocks[-1] = tied[:2]
    blocks[1:-1] = tied[2:]
    blocks[-1] = exchange(team_size - 1)

    rows_of = place_rows(
        chosen_experts, capacity, fallback, local_experts, slot_cap, spill_peer, peer_count
    )
    hit = rows_of[:, :, None] == jnp.arange(row_count, dtype=jnp.int32)[None, None, :]
    spread = jnp.any(hit, axis=1).astype(jnp.bfloat16)
    weight = jnp.sum(jnp.where(hit, combine_weights[:, :, None], 0.0), axis=1)

    for_partner = dot32(partner_tokens, down_half).astype(jnp.bfloat16)
    from_partner = swap(for_partner)
    for_me = dot32(tokens, down_half).astype(jnp.bfloat16)
    latent = ordered(for_me, from_partner, 1)
    outgoing = lax.dot_general(
        spread, latent, (((0,), (0,)), ((), ())), preferred_element_type=jnp.float32
    ).astype(jnp.bfloat16)
    outgoing = outgoing.reshape(local_experts * peer_count, slot_width, latent_width)
    arrived = lax.all_to_all(outgoing, ALL, split_axis=0, concat_axis=0, tiled=True)
    arrived, up_pair, blocks[-1] = lax.optimization_barrier((arrived, up_pair, blocks[-1]))
    groups = local_experts * peer_count
    units = expert_down.shape[1]
    weight = weight.reshape(tok_count, groups, slot_width)
    cut = slot_width // 2
    up_half = gather(up_pair)
    combined = jnp.zeros((tok_count, latent_width), jnp.float32)
    for low, high in ((0, cut), (cut, slot_width)):
        rows = arrived[:, low:high].reshape(-1, latent_width)
        total = jnp.zeros(rows.shape, jnp.float32)
        for part in blocks:
            both = dot32(rows, part[:latent_width])
            hidden = (jax.nn.silu(both[:, :units]) * both[:, units:]).astype(jnp.bfloat16)
            term = dot32(hidden, part[latent_width:]).astype(jnp.bfloat16)
            total = total + term.astype(jnp.float32)
        served = total.astype(jnp.bfloat16).reshape(groups, high - low, latent_width)
        back = lax.all_to_all(served, ALL, split_axis=0, concat_axis=0, tiled=True)
        back = back.reshape(-1, latent_width)
        share = weight[:, :, low:high].reshape(tok_count, -1)
        share_high = share.astype(jnp.bfloat16)
        share_low = (share - share_high.astype(jnp.float32)).astype(jnp.bfloat16)
        combined = combined + dot32(share_high, back) + dot32(share_low, back)
    combined = combined.astype(jnp.bfloat16)

    up_other = swap(up_half)
    mine = dot32(combined, up_half).astype(jnp.bfloat16)
    other = dot32(combined, up_other).astype(jnp.bfloat16)
    return ordered(mine, other, 1)


def solution(mesh):
    teams, peers = mesh.devices.shape
    split = Mesh(mesh.devices.reshape(teams, peers // 2, 2), ALL)
    experts = ("pair", "core")
    mapped = jax.shard_map(
        on_device,
        mesh=split,
        in_specs=(
            P(ALL, None),
            P(ALL, None),
            P(ALL, None),
            P(experts, None, "dp"),
            P(experts, None, "dp"),
            P(experts, "dp", None),
            P(ALL, None),
            P(ALL, None),
            P(),
            P(ALL, None),
        ),
        out_specs=P(ALL, None),
        check_vma=False,
    )
    return mapped
```

```python
import jax
import jax.numpy as jnp
from jax import lax
from jax.sharding import Mesh
from jax.sharding import PartitionSpec as P

ALL = ("dp", "pair", "core")
PLANE = ("dp", "pair")


def dot32(a, b):
    return jnp.dot(a, b, preferred_element_type=jnp.float32)


def place_rows(block_experts, capacity, fallback, local_experts, slot_cap, spill_peer, peer_count):
    flat_experts = block_experts.reshape(-1)
    expert_count = capacity.shape[0]
    onehot = (flat_experts[:, None] == jnp.arange(expert_count, dtype=jnp.int32)[None, :]).astype(
        jnp.int32
    )
    earlier = jnp.cumsum(onehot, axis=0) - onehot
    slot_rank = jnp.sum(earlier * onehot, axis=1)
    slot_limit = jnp.sum(onehot * capacity[None, :], axis=1)
    is_main = slot_rank < slot_limit
    overflow = jnp.where(is_main, 0, 1).astype(jnp.int32)
    spill_number = jnp.cumsum(overflow) - overflow
    spill_all = spill_peer * peer_count
    in_spill = spill_number < spill_all
    number_hot = spill_number[:, None] == jnp.arange(spill_all, dtype=jnp.int32)[None, :]
    spill_target = jnp.sum(jnp.where(number_hot, fallback.reshape(1, -1), 0), axis=1)
    target = jnp.where(is_main, flat_experts, spill_target)
    slot = jnp.where(is_main, slot_rank, slot_cap + spill_number // peer_count)
    slot_width = slot_cap + spill_peer
    row = ((target % local_experts) * peer_count + target // local_experts) * slot_width + slot
    outside = local_experts * peer_count * slot_width
    return jnp.where(is_main | in_spill, row, outside).reshape(block_experts.shape)


def on_device(
    tokens,
    latent_down,
    latent_up,
    expert_gate,
    expert_up,
    expert_down,
    chosen_experts,
    combine_weights,
    capacity,
    fallback,
):
    tok_count = tokens.shape[0]
    latent_width = expert_gate.shape[1]
    local_experts = expert_gate.shape[0]
    top_count = chosen_experts.shape[1]
    peer_count = lax.axis_size("pair") * lax.axis_size("core")
    team_size = lax.axis_size("dp")
    expert_count = capacity.shape[0]
    spill_peer = fallback.shape[1] // peer_count
    slot_cap = tok_count * top_count // expert_count
    slot_width = slot_cap + spill_peer
    row_count = local_experts * peer_count * slot_width
    team = lax.axis_index("dp")
    core = lax.axis_index("core")

    def swap(value):
        return lax.ppermute(value, "core", [(0, 1), (1, 0)])

    def ordered(mine, other, axis):
        first = jnp.where(core == 0, mine, other)
        second = jnp.where(core == 0, other, mine)
        return jnp.concatenate([first, second], axis=axis)

    def column_half(shard):
        half = shard.shape[1] // 2
        mine = lax.dynamic_slice_in_dim(shard, core * half, half, 1)
        other = swap(lax.dynamic_slice_in_dim(shard, (1 - core) * half, half, 1))
        return ordered(mine, other, 0)

    def gather(half):
        return lax.all_gather(half, PLANE, axis=0, tiled=True)

    down_half = gather(column_half(latent_down))
    up_pair = column_half(latent_up)
    partner_tokens = swap(tokens)

    blocks = []
    for shift in range(team_size):
        partner = jnp.bitwise_xor(team, shift)
        gate, up, down = (
            lax.dynamic_index_in_dim(w, partner, 0, keepdims=False)
            for w in (expert_gate, expert_up, expert_down)
        )
        part = jnp.concatenate([jnp.concatenate([gate, up], axis=1), down], axis=0)
        blocks.append(part)

    def exchange(shift):
        pairs = [(d, d ^ shift) for d in range(team_size)]
        return lax.ppermute(blocks[shift], "dp", pairs)

    early = range(1, team_size - 1)
    tied = lax.optimization_barrier((down_half, blocks[-1], *[exchange(s) for s in early]))
    down_half, blocks[-1] = tied[:2]
    blocks[1:-1] = tied[2:]
    last_pairs = [(d, d ^ (team_size - 1)) for d in range(team_size)]
    last_in = lax.ppermute(blocks[-1][:latent_width], "dp", last_pairs)
    last_out = lax.ppermute(blocks[-1][latent_width:], "dp", last_pairs)

    rows_of = place_rows(
        chosen_experts, capacity, fallback, local_experts, slot_cap, spill_peer, peer_count
    )
    hit = rows_of[:, :, None] == jnp.arange(row_count, dtype=jnp.int32)[None, None, :]
    spread = jnp.any(hit, axis=1).astype(jnp.bfloat16)
    weight = jnp.sum(jnp.where(hit, combine_weights[:, :, None], 0.0), axis=1)

    for_partner = dot32(partner_tokens, down_half).astype(jnp.bfloat16)
    from_partner = swap(for_partner)
    for_me = dot32(tokens, down_half).astype(jnp.bfloat16)
    latent = ordered(for_me, from_partner, 1)
    outgoing = lax.dot_general(
        spread, latent, (((0,), (0,)), ((), ())), preferred_element_type=jnp.float32
    ).astype(jnp.bfloat16)
    outgoing = outgoing.reshape(local_experts * peer_count, slot_width, latent_width)
    outgoing, up_pair = lax.optimization_barrier((outgoing, up_pair))
    arrived = lax.all_to_all(outgoing, ALL, split_axis=0, concat_axis=0, tiled=True)
    arrived, last_in = lax.optimization_barrier((arrived, last_in))
    halves = [(part[:latent_width], part[latent_width:]) for part in blocks[:-1]]
    halves.append((last_in, last_out))
    groups = local_experts * peer_count
    units = expert_down.shape[1]
    weight = weight.reshape(tok_count, groups, slot_width)
    cut = slot_width // 2
    up_half = gather(up_pair)
    combined = jnp.zeros((tok_count, latent_width), jnp.float32)
    for low, high in ((0, cut), (cut, slot_width)):
        rows = arrived[:, low:high].reshape(-1, latent_width)
        total = jnp.zeros(rows.shape, jnp.float32)
        for inward, outward in halves:
            both = dot32(rows, inward)
            hidden = (jax.nn.silu(both[:, :units]) * both[:, units:]).astype(jnp.bfloat16)
            term = dot32(hidden, outward).astype(jnp.bfloat16)
            total = total + term.astype(jnp.float32)
        served = total.astype(jnp.bfloat16).reshape(groups, high - low, latent_width)
        back = lax.all_to_all(served, ALL, split_axis=0, concat_axis=0, tiled=True)
        back = back.reshape(-1, latent_width)
        share = weight[:, :, low:high].reshape(tok_count, -1)
        share_high = share.astype(jnp.bfloat16)
        share_low = (share - share_high.astype(jnp.float32)).astype(jnp.bfloat16)
        combined = combined + dot32(share_high, back) + dot32(share_low, back)
    combined = combined.astype(jnp.bfloat16)

    up_other = swap(up_half)
    mine = dot32(combined, up_half).astype(jnp.bfloat16)
    other = dot32(combined, up_other).astype(jnp.bfloat16)
    return ordered(mine, other, 1)


def solution(mesh):
    teams, peers = mesh.devices.shape
    split = Mesh(mesh.devices.reshape(teams, peers // 2, 2), ALL)
    experts = ("pair", "core")
    mapped = jax.shard_map(
        on_device,
        mesh=split,
        in_specs=(
            P(ALL, None),
            P(ALL, None),
            P(ALL, None),
            P(experts, None, "dp"),
            P(experts, None, "dp"),
            P(experts, "dp", None),
            P(ALL, None),
            P(ALL, None),
            P(),
            P(ALL, None),
        ),
        out_specs=P(ALL, None),
        check_vma=False,
    )
    return mapped
```

```python
import jax
import jax.numpy as jnp
from jax import lax
from jax.sharding import Mesh
from jax.sharding import PartitionSpec as P

ALL = ("dp", "pair", "core")
PLANE = ("dp", "pair")


def dot32(a, b):
    return jnp.dot(a, b, preferred_element_type=jnp.float32)


def place_rows(block_experts, capacity, fallback, local_experts, slot_cap, spill_peer, peer_count):
    flat_experts = block_experts.reshape(-1)
    expert_count = capacity.shape[0]
    onehot = (flat_experts[:, None] == jnp.arange(expert_count, dtype=jnp.int32)[None, :]).astype(
        jnp.int32
    )
    earlier = jnp.cumsum(onehot, axis=0) - onehot
    slot_rank = jnp.sum(earlier * onehot, axis=1)
    slot_limit = jnp.sum(onehot * capacity[None, :], axis=1)
    is_main = slot_rank < slot_limit
    overflow = jnp.where(is_main, 0, 1).astype(jnp.int32)
    spill_number = jnp.cumsum(overflow) - overflow
    spill_all = spill_peer * peer_count
    in_spill = spill_number < spill_all
    number_hot = spill_number[:, None] == jnp.arange(spill_all, dtype=jnp.int32)[None, :]
    spill_target = jnp.sum(jnp.where(number_hot, fallback.reshape(1, -1), 0), axis=1)
    target = jnp.where(is_main, flat_experts, spill_target)
    slot = jnp.where(is_main, slot_rank, slot_cap + spill_number // peer_count)
    slot_width = slot_cap + spill_peer
    row = ((target % local_experts) * peer_count + target // local_experts) * slot_width + slot
    outside = local_experts * peer_count * slot_width
    return jnp.where(is_main | in_spill, row, outside).reshape(block_experts.shape)


def on_device(
    tokens,
    latent_down,
    latent_up,
    expert_gate,
    expert_up,
    expert_down,
    chosen_experts,
    combine_weights,
    capacity,
    fallback,
):
    tok_count = tokens.shape[0]
    latent_width = expert_gate.shape[1]
    local_experts = expert_gate.shape[0]
    top_count = chosen_experts.shape[1]
    peer_count = lax.axis_size("pair") * lax.axis_size("core")
    team_size = lax.axis_size("dp")
    expert_count = capacity.shape[0]
    spill_peer = fallback.shape[1] // peer_count
    slot_cap = tok_count * top_count // expert_count
    slot_width = slot_cap + spill_peer
    row_count = local_experts * peer_count * slot_width
    team = lax.axis_index("dp")
    core = lax.axis_index("core")

    def swap(value):
        return lax.ppermute(value, "core", [(0, 1), (1, 0)])

    def ordered(mine, other, axis):
        first = jnp.where(core == 0, mine, other)
        second = jnp.where(core == 0, other, mine)
        return jnp.concatenate([first, second], axis=axis)

    def column_half(shard):
        half = shard.shape[1] // 2
        mine = lax.dynamic_slice_in_dim(shard, core * half, half, 1)
        other = swap(lax.dynamic_slice_in_dim(shard, (1 - core) * half, half, 1))
        return ordered(mine, other, 0)

    def gather(half):
        return lax.all_gather(half, PLANE, axis=0, tiled=True)

    down_half = gather(column_half(latent_down))
    up_pair = column_half(latent_up)
    partner_tokens = swap(tokens)

    blocks = []
    for shift in range(team_size):
        partner = jnp.bitwise_xor(team, shift)
        gate, up, down = (
            lax.dynamic_index_in_dim(w, partner, 0, keepdims=False)
            for w in (expert_gate, expert_up, expert_down)
        )
        part = jnp.concatenate([jnp.concatenate([gate, up], axis=1), down], axis=0)
        blocks.append(part)

    def exchange(shift):
        pairs = [(d, d ^ shift) for d in range(team_size)]
        return lax.ppermute(blocks[shift], "dp", pairs)

    early = range(1, team_size - 1)
    arriving = [exchange(s) for s in early]

    rows_of = place_rows(
        chosen_experts, capacity, fallback, local_experts, slot_cap, spill_peer, peer_count
    )
    hit = rows_of[:, :, None] == jnp.arange(row_count, dtype=jnp.int32)[None, None, :]
    spread = jnp.any(hit, axis=1).astype(jnp.bfloat16)
    weight = jnp.sum(jnp.where(hit, combine_weights[:, :, None], 0.0), axis=1)

    for_partner = dot32(partner_tokens, down_half).astype(jnp.bfloat16)
    from_partner = swap(for_partner)
    for_me = dot32(tokens, down_half).astype(jnp.bfloat16)
    latent = ordered(for_me, from_partner, 1)
    outgoing = lax.dot_general(
        spread, latent, (((0,), (0,)), ((), ())), preferred_element_type=jnp.float32
    ).astype(jnp.bfloat16)
    outgoing = outgoing.reshape(local_experts * peer_count, slot_width, latent_width)
    tied = lax.optimization_barrier((outgoing, up_pair, blocks[-1], *arriving))
    outgoing, up_pair, blocks[-1] = tied[:3]
    blocks[1:-1] = tied[3:]
    last_pairs = [(d, d ^ (team_size - 1)) for d in range(team_size)]
    last_in = lax.ppermute(blocks[-1][:latent_width], "dp", last_pairs)
    last_out = lax.ppermute(blocks[-1][latent_width:], "dp", last_pairs)
    arrived = lax.all_to_all(outgoing, ALL, split_axis=0, concat_axis=0, tiled=True)
    arrived, last_in = lax.optimization_barrier((arrived, last_in))
    halves = [(part[:latent_width], part[latent_width:]) for part in blocks[:-1]]
    halves.append((last_in, last_out))
    groups = local_experts * peer_count
    units = expert_down.shape[1]
    weight = weight.reshape(tok_count, groups, slot_width)
    cut = slot_width // 2
    up_half = gather(up_pair)
    combined = jnp.zeros((tok_count, latent_width), jnp.float32)
    for low, high in ((0, cut), (cut, slot_width)):
        rows = arrived[:, low:high].reshape(-1, latent_width)
        total = jnp.zeros(rows.shape, jnp.float32)
        for inward, outward in halves:
            both = dot32(rows, inward)
            hidden = (jax.nn.silu(both[:, :units]) * both[:, units:]).astype(jnp.bfloat16)
            term = dot32(hidden, outward).astype(jnp.bfloat16)
            total = total + term.astype(jnp.float32)
        served = total.astype(jnp.bfloat16).reshape(groups, high - low, latent_width)
        back = lax.all_to_all(served, ALL, split_axis=0, concat_axis=0, tiled=True)
        back = back.reshape(-1, latent_width)
        share = weight[:, :, low:high].reshape(tok_count, -1)
        share_high = share.astype(jnp.bfloat16)
        share_low = (share - share_high.astype(jnp.float32)).astype(jnp.bfloat16)
        combined = combined + dot32(share_high, back) + dot32(share_low, back)
    combined = combined.astype(jnp.bfloat16)

    up_other = swap(up_half)
    mine = dot32(combined, up_half).astype(jnp.bfloat16)
    other = dot32(combined, up_other).astype(jnp.bfloat16)
    return ordered(mine, other, 1)


def solution(mesh):
    teams, peers = mesh.devices.shape
    split = Mesh(mesh.devices.reshape(teams, peers // 2, 2), ALL)
    experts = ("pair", "core")
    mapped = jax.shard_map(
        on_device,
        mesh=split,
        in_specs=(
            P(ALL, None),
            P(ALL, None),
            P(ALL, None),
            P(experts, None, "dp"),
            P(experts, None, "dp"),
            P(experts, "dp", None),
            P(ALL, None),
            P(ALL, None),
            P(),
            P(ALL, None),
        ),
        out_specs=P(ALL, None),
        check_vma=False,
    )
    return mapped
```
